32 devices in a mesh: grp: 4 (over x, core), row: 8 (over z, y).
Axes of the slice: x: 2, y: 2, z: 4, core: 2. Of those that a mesh axis runs over, the one named last changes fastest.
Arguments:
- inputs: bfloat16 [16384, 2048], P(('grp', 'row')), may hold values from -6 to 6
- norm_gain: float32 [2048], replicated, may hold values from 0.25 to 1.75
- w_hidden: bfloat16 [2048, 2048], replicated, may hold values from -0.125 to 0.125
- w_proj: bfloat16 [2048, 256], replicated, may hold values from -0.125 to 0.125
- observed: float32 [16384], P(('grp', 'row')), may hold values from -6 to 6
- evolved: float32 [16384], P(('grp', 'row')), may hold values from -6 to 6
- station_ids: int32 [16384], P(('grp', 'row')), may hold values from 0 to 511
- station_gain: float32 [512], replicated, may hold values from 0.3 to 3
- station_offset: float32 [512], replicated, may hold values from -4 to 4
Outputs:
- grad_hidden: float32 [2048, 2048], P(('grp', 'row'))
- grad_proj: float32 [2048, 256], P(('grp', 'row'))
The draws below stay inside these ranges and needn't reach their ends.
Inputs may be any that keep to these rules, and one draw needn't show every extreme that they name: `station_ids`: a station number for every row.
All inputs are finite; a program needn't handle non-finite values.
Results may differ from the reference program's by a relative error of at most 0.0068.
Values sent between devices are 32-bit elements; how exact they have to be, the bound alone decides.
A program may use at most 128 MiB of HBM per device.

```python
import math
import jax
import jax.numpy as jnp
from jax import lax

W = 2048
F = 256
STATIONS = 512
ROWS = 16384


def plant(result, rng, low, high):
    shape = result.shape
    place = [jax.random.randint(jax.random.fold_in(rng, axis), (), 0, shape[axis]) for axis in range(len(shape))]
    result = result.at[tuple(place)].set(low)
    longest = shape.index(max(shape))
    place[longest] = (place[longest] + 1) % shape[longest]
    return result.at[tuple(place)].set(high)


def level_of(key, shape, pieces, smallest, top_value):
    level = 1.0
    for position, blocks in pieces:
        heights = jax.random.uniform(jax.random.fold_in(jax.random.fold_in(key, 6), position), (blocks,), jnp.float32, smallest / len(pieces), top_value / len(pieces))
        level = level * jnp.repeat(jnp.exp(heights), shape[position] // blocks).reshape((-1,) + (1,) * (len(shape) - 1 - position))
    return level


def centred(rng, extent, deviation, limit, shards=(), kind=jnp.bfloat16):
    values = deviation * jax.random.normal(rng, extent, jnp.float32)
    if shards:
        values = values * level_of(rng, extent, shards, -0.22, 0.18)
    return jnp.clip(values, -limit, limit).astype(kind)


def setup_inputs(seed: int = 0) -> dict:
    key_list = jax.random.split(jax.random.key(seed), 10)
    inputs = centred(key_list[0], (ROWS, W), 1.0, 6.0, ((0, 32),))
    norm_gain = jnp.clip(1.0 + 0.15 * jax.random.normal(key_list[1], (W,), jnp.float32), 0.25, 1.75)
    w_hidden = centred(key_list[2], (W, W), W ** -0.5, 0.125)
    w_proj = centred(key_list[3], (W, F), W ** -0.5, 0.125)
    observed = centred(key_list[4], (ROWS,), 1.0, 6.0, ((0, 32),), jnp.float32)
    evolved = centred(key_list[5], (ROWS,), 1.0, 6.0, ((0, 32),), jnp.float32)
    station_ids = plant(jax.random.randint(key_list[6], (ROWS,), 0, STATIONS), jax.random.fold_in(key_list[6], 1), 0, STATIONS - 1).astype(jnp.int32)
    station_gain = jnp.clip(jnp.exp(jax.random.uniform(key_list[7], (STATIONS,), jnp.float32, math.log(0.3), math.log(3.0))), 0.3, 3.0)
    station_offset = centred(key_list[8], (STATIONS,), 1.0, 4.0, (), jnp.float32)
    return {"inputs": inputs, "norm_gain": norm_gain, "w_hidden": w_hidden, "w_proj": w_proj, "observed": observed, "evolved": evolved, "station_ids": station_ids, "station_gain": station_gain, "station_offset": station_offset}


def forward(rows_in, norm_gain, w_hidden, w_proj):
    values = rows_in.astype(jnp.float32)
    mean_square = lax.optimization_barrier(jnp.mean(values * values, axis=1, keepdims=True))
    normed = (values * lax.rsqrt(mean_square + 1e-06) * norm_gain).astype(jnp.bfloat16)
    pre = jnp.dot(normed.astype(jnp.float32), w_hidden.astype(jnp.float32), preferred_element_type=jnp.float32)
    hidden = (values + jax.nn.silu(pre)).astype(jnp.bfloat16)
    features = jnp.dot(hidden.astype(jnp.float32), w_proj.astype(jnp.float32), preferred_element_type=jnp.float32)
    return (normed, pre, hidden, features)

def make_target(observed, evolved, station_ids, station_gain, station_offset):
    onehot = (station_ids[:, None] == jnp.arange(station_gain.shape[0], dtype=jnp.int32)[None, :]).astype(jnp.float32)
    gain_rows = jnp.dot(onehot, station_gain, precision=lax.Precision.HIGHEST)
    offset_rows = jnp.dot(onehot, station_offset, precision=lax.Precision.HIGHEST)
    return observed - gain_rows * evolved - offset_rows

def contract_rows(left, right, precision=None):
    return lax.dot_general(left.astype(jnp.float32), right.astype(jnp.float32), (((0,), (0,)), ((), ())), precision=precision, preferred_element_type=jnp.float32)

def reference(inputs, norm_gain, w_hidden, w_proj, observed, evolved, station_ids, station_gain, station_offset):
    total = inputs.shape[0]
    width = inputs.shape[1]
    feat_width = w_proj.shape[1]
    block_rows = math.gcd(total, 4096)
    num_blocks = total // block_rows
    xs = (inputs.reshape(num_blocks, block_rows, width), observed.reshape(num_blocks, block_rows), evolved.reshape(num_blocks, block_rows), station_ids.reshape(num_blocks, block_rows))

    def first_pass(carry, item):
        rows_in, obs_blk, sim_blk, ids_blk = item
        features = forward(rows_in, norm_gain, w_hidden, w_proj)[3]
        target = make_target(obs_blk, sim_blk, ids_blk, station_gain, station_offset)
        gram = carry[0] + contract_rows(features, features, lax.Precision.HIGHEST)
        moment = carry[1] + contract_rows(features, target[:, None], lax.Precision.HIGHEST)[:, 0]
        return ((gram, moment), None)
    init = (jnp.zeros((feat_width, feat_width), jnp.float32), jnp.zeros((feat_width,), jnp.float32))
    (gram, moment), unused = lax.scan(first_pass, init, xs)
    gram = gram + jnp.eye(feat_width, dtype=jnp.float32)
    factor = jnp.linalg.cholesky(gram)
    posterior = jax.scipy.linalg.cho_solve((factor, True), moment)

    def second_pass(carry, item):
        rows_in, obs_blk, sim_blk, ids_blk = item
        normed, pre, hidden, features = forward(rows_in, norm_gain, w_hidden, w_proj)
        target = make_target(obs_blk, sim_blk, ids_blk, station_gain, station_offset)
        resid = jnp.dot(features, posterior, precision=lax.Precision.HIGHEST) - target
        feat_grad = (resid[:, None] * posterior[None, :]).astype(jnp.bfloat16)
        row_moment = carry[1] + contract_rows(hidden.astype(jnp.float32), resid[:, None], lax.Precision.HIGHEST)[:, 0]
        back = lax.dot_general(feat_grad.astype(jnp.float32), w_proj.astype(jnp.float32), (((1,), (1,)), ((), ())), preferred_element_type=jnp.float32)
        sigmoid_pre = jax.nn.sigmoid(pre)
        pre_grad = (back * sigmoid_pre * (1.0 + pre * (1.0 - sigmoid_pre))).astype(jnp.bfloat16)
        grad_hidden = carry[0] + contract_rows(normed, pre_grad)
        return ((grad_hidden, row_moment), None)
    init_two = (jnp.zeros((width, width), jnp.float32), jnp.zeros((width,), jnp.float32))
    (grad_hidden, row_moment), unused_two = lax.scan(second_pass, init_two, xs)
    grad_proj = row_moment[:, None] * posterior[None, :]
    return (grad_hidden, grad_proj)
```

```python
import functools

import jax
import jax.numpy as jnp
from jax import lax
from jax.experimental import pallas as pl
from jax.experimental.pallas import tpu as pltpu
from jax.sharding import PartitionSpec as P

HIGH = lax.Precision.HIGHEST
MESH = pl.DeviceIdType.MESH
VMEM = pl.BlockSpec(memory_space=pltpu.VMEM)


def forward(rows_in, norm_gain, w_hidden, w_proj):
    values = rows_in.astype(jnp.float32)
    mean_square = jnp.mean(values * values, axis=1, keepdims=True)
    normed = (values * lax.rsqrt(mean_square + 1e-06) * norm_gain).astype(jnp.bfloat16)
    pre = jnp.dot(normed, w_hidden, preferred_element_type=jnp.float32)
    hidden = (values + jax.nn.silu(pre)).astype(jnp.bfloat16)
    features = jnp.dot(hidden, w_proj, preferred_element_type=jnp.float32)
    return (normed, pre, hidden, features)


def make_target(observed, evolved, station_ids, station_gain, station_offset):
    onehot = (
        station_ids[:, None] == jnp.arange(station_gain.shape[0], dtype=jnp.int32)[None, :]
    ).astype(jnp.float32)
    gain_rows = jnp.dot(onehot, station_gain, precision=HIGH)
    offset_rows = jnp.dot(onehot, station_offset, precision=HIGH)
    return observed - gain_rows * evolved - offset_rows


def contract_rows(left, right, precision=None):
    return lax.dot_general(
        left,
        right,
        (((0,), (0,)), ((), ())),
        precision=precision,
        preferred_element_type=jnp.float32,
    )


def reduce_kernel(groups, rows, part, out, landed, send_a, recv_a, send_b, recv_b):
    count = groups * rows
    me = lax.axis_index("grp") * rows + lax.axis_index("row")

    def peer(step):
        where = lax.rem(me + step, count)
        return where, (where // rows, lax.rem(where, rows))

    barrier = pltpu.get_barrier_semaphore()

    @pl.loop(1, count)
    def _(step):
        pl.semaphore_signal(barrier, inc=1, device_id=peer(step)[1], device_id_type=MESH)

    pl.semaphore_wait(barrier, count - 1)

    def scatter(step):
        where, device = peer(step)
        return pltpu.make_async_remote_copy(
            src_ref=part.at[where],
            dst_ref=landed.at[step],
            send_sem=send_a.at[step],
            recv_sem=recv_a.at[step],
            device_id=device,
            device_id_type=MESH,
        )

    def gather(step):
        return pltpu.make_async_remote_copy(
            src_ref=out.at[me],
            dst_ref=out.at[me],
            send_sem=send_b.at[step],
            recv_sem=recv_b.at[step],
            device_id=peer(step)[1],
            device_id_type=MESH,
        )

    @pl.loop(1, count)
    def _(step):
        scatter(step).start()

    def add(step, total):
        scatter(step).wait_recv()
        return total + landed[step]

    out[me] = lax.fori_loop(1, count, add, part[me])

    @pl.loop(1, count)
    def _(step):
        gather(step).start()

    @pl.loop(1, count)
    def _(step):
        scatter(step).wait_send()
        gather(step).wait()


def reduce_all(part, groups, rows):
    count = groups * rows
    high, wide = part.shape
    blocks = part.reshape(count, high // count, wide)
    out = pl.pallas_call(
        functools.partial(reduce_kernel, groups, rows),
        out_shape=jax.ShapeDtypeStruct(blocks.shape, jnp.float32),
        in_specs=[VMEM],
        out_specs=VMEM,
        scratch_shapes=[pltpu.VMEM(blocks.shape, jnp.float32)]
        + [pltpu.SemaphoreType.DMA((count,))] * 4,
        compiler_params=pltpu.CompilerParams(
            collective_id=0, has_side_effects=True, vmem_limit_bytes=16 * 2**20
        ),
    )(blocks)
    return out.reshape(high, wide)


def solve_kernel(aug, out, work):
    feat, wide = aug.shape
    rows = lax.broadcasted_iota(jnp.int32, (feat, wide), 0)
    columns = lax.broadcasted_iota(jnp.int32, (feat, wide), 1)
    work[...] = aug[...] + jnp.where(rows == columns, 1.0, 0.0)
    tall = 8
    sub = lax.broadcasted_iota(jnp.int32, (tall, 1), 0)
    for k in range(feat // tall):
        low = k * tall
        base = low // 128 * 128
        pivot = work[low : low + tall, base:]
        for i in range(tall):
            lane = low + i - base
            column = pivot[:, lane : lane + 1]
            line = pivot[i : i + 1, :] * (1.0 / column[i : i + 1, :])
            pivot = jnp.where(sub == i, line, pivot - column * line)
        for t in list(range(k + 1, feat // tall)) + list(range(k)):
            here = slice(t * tall, (t + 1) * tall)
            left = work[here, low : low + tall]
            total = work[here, base:]
            for i in range(tall):
                total = total - left[:, i : i + 1] * pivot[i : i + 1, :]
            work[here, base:] = total
        work[low : low + tall, base:] = pivot
    out[...] = work[:, feat:]


def solve(aug):
    feat, wide = aug.shape
    return pl.pallas_call(
        solve_kernel,
        out_shape=jax.ShapeDtypeStruct((feat, wide - feat), jnp.float32),
        in_specs=[VMEM],
        out_specs=VMEM,
        scratch_shapes=[pltpu.VMEM((feat, wide), jnp.float32)],
        compiler_params=pltpu.CompilerParams(vmem_limit_bytes=40 * 2**20),
    )(aug)


def scatter_kernel(side, depth, pieces, left, right, extra, out, extra_out, *scratch):
    main, small, (send_sem, recv_sem) = scratch[:6], scratch[6:12], scratch[12:]
    grp, row = lax.axis_index("grp"), lax.axis_index("row")
    core, x = lax.rem(grp, 2), grp // 2
    z, y = row // side, lax.rem(row, side)
    p = x + core * (y - x)
    q = y + core * (x - y)
    size = out.shape[1] // pieces

    def device(new_p, new_q, new_z, new_core):
        new_x = new_p + core * (new_q - new_p)
        new_y = new_q + core * (new_p - new_q)
        return (new_x * 2 + new_core, new_z * side + new_y)

    hops = [[(0, None, device(p, q, z, 1 - core))], [], [], []]
    for step in range(1, side):
        there = lax.rem(p + step, side)
        hops[1].append((step - 1, there, device(there, q, z, core)))
    for step in range(1, side):
        there = lax.rem(q + step, side)
        hops[2].append((step - 1, there, device(p, there, z, core)))
    for step in range(1, depth):
        there = lax.rem(z + step, depth)
        hops[3].append((step - 1, there, device(p, q, there, core)))

    barrier = pltpu.get_barrier_semaphore()
    for hop in sum(hops, []):
        pl.semaphore_signal(barrier, inc=1, device_id=hop[2], device_id_type=MESH)
    pl.semaphore_wait(barrier, sum(len(stage) for stage in hops))

    def copies(group, piece, stage):
        give, mine, land = group[0], group[1], group[2:]
        sem = pieces if group is small else piece
        number = sum(len(before) for before in hops[:stage])
        result = []
        for slot, there, target in hops[stage]:
            if stage == 0:
                src, dst = give.at[piece], land[0].at[piece]
            elif stage == 1:
                src, dst = mine.at[piece, there], land[1].at[piece, slot]
            elif stage == 2:
                src, dst = mine.at[piece, p, there], land[2].at[piece, slot]
            else:
                src, dst = mine.at[piece, p, q, there], land[3].at[piece, slot]
            result.append(
                pltpu.make_async_remote_copy(
                    src_ref=src,
                    dst_ref=dst,
                    send_sem=send_sem.at[sem, number + slot],
                    recv_sem=recv_sem.at[sem, number + slot],
                    device_id=target,
                    device_id_type=MESH,
                )
            )
        return result

    def begin(group, piece, stage):
        for copy in copies(group, piece, stage):
            copy.start()

    def finish(group, piece, stage):
        mine, land = group[1], group[2:]
        for copy in copies(group, piece, stage):
            copy.wait_recv()
        if stage == 0:
            mine[piece] = mine[piece] + land[0][piece]
        elif stage == 1:
            for slot in range(side - 1):
                mine[piece, p] = mine[piece, p] + land[1][piece, slot]
        elif stage == 2:
            for slot in range(side - 1):
                mine[piece, p, q] = mine[piece, p, q] + land[2][piece, slot]
        else:
            total = mine[piece, p, q, z]
            for slot in range(depth - 1):
                total = total + land[3][piece, slot]
            if group is small:
                extra_out[...] = total
            else:
                out[:, pl.ds(pl.multiple_of(piece * size, size), size)] = total
        if stage < 3:
            begin(group, piece, stage + 1)

    def product(half, piece, into):
        columns = pl.ds(pl.multiple_of(piece * size, size), size)
        into[piece] = jnp.dot(
            left[half], right[:, columns], preferred_element_type=jnp.float32
        ).reshape(into.shape[1:])

    small[0][0] = extra[1 - core]
    small[1][0] = extra[core]
    begin(small, 0, 0)

    @pl.loop(0, pieces)
    def _(piece):
        product(1 - core, piece, main[0])
        begin(main, piece, 0)
        product(core, piece, main[1])

        @pl.when(piece > 0)
        def _():
            finish(main, piece - 1, 0)

    finish(main, pieces - 1, 0)
    finish(small, 0, 0)
    finish(small, 0, 1)

    @pl.loop(0, pieces)
    def _(piece):
        finish(main, piece, 1)

        @pl.when(piece > 0)
        def _():
            finish(main, piece - 1, 2)

    finish(main, pieces - 1, 2)
    finish(small, 0, 2)
    finish(small, 0, 3)

    @pl.loop(0, pieces)
    def _(piece):
        finish(main, piece, 3)

    for stage in range(4):
        for copy in copies(small, 0, stage):
            copy.wait_send()

    @pl.loop(0, pieces)
    def _(piece):
        for stage in range(4):
            for copy in copies(main, piece, stage):
                copy.wait_send()


def order_rows(array, side, depth):
    tail = array.shape[1:]
    split = array.reshape((side, 2, depth, side, -1) + tail)
    rest = tuple(range(3, split.ndim - 1))
    first = jnp.transpose(split[:, 0], (0, 2, 1) + rest)
    second = jnp.transpose(split[:, 1], (2, 0, 1) + rest)
    return jnp.stack([first, second])


def scatter_sum(normed, pre_grad, moment_term, groups, rows):
    side = groups // 2
    depth = rows // side
    own = normed.shape[1] // (groups * rows)
    width = pre_grad.shape[1]
    pieces = width // 256
    left = order_rows(normed.T, side, depth).reshape(2, -1, normed.shape[0])
    extra = order_rows(moment_term, side, depth)[..., None, :]
    extra = jnp.pad(extra, [(0, 0)] * 4 + [(0, 7), (0, 128 - own)])

    def stage_buffers(count, high, wide):
        full = (count, side, side, depth, high, wide)
        shapes = [full] * 3 + [
            (count, side - 1, side, depth, high, wide),
            (count, side - 1, depth, high, wide),
            (count, depth - 1, high, wide),
        ]
        return [pltpu.VMEM(shape, jnp.float32) for shape in shapes]

    number = 1 + 2 * (side - 1) + depth - 1
    return pl.pallas_call(
        functools.partial(scatter_kernel, side, depth, pieces),
        out_shape=(
            jax.ShapeDtypeStruct((own, width), jnp.float32),
            jax.ShapeDtypeStruct((8, 128), jnp.float32),
        ),
        in_specs=[VMEM] * 3,
        out_specs=(VMEM, VMEM),
        scratch_shapes=stage_buffers(pieces, own, width // pieces)
        + stage_buffers(1, 8, 128)
        + [pltpu.SemaphoreType.DMA((pieces + 1, number))] * 2,
        compiler_params=pltpu.CompilerParams(
            collective_id=1, has_side_effects=True, vmem_limit_bytes=56 * 2**20
        ),
    )(left, pre_grad, extra)


def body(
    inputs,
    norm_gain,
    w_hidden,
    w_proj,
    observed,
    evolved,
    station_ids,
    station_gain,
    station_offset,
):
    groups, rows = lax.axis_size("grp"), lax.axis_size("row")
    feat_width = w_proj.shape[1]
    normed, pre, hidden, features = forward(inputs, norm_gain, w_hidden, w_proj)
    target = make_target(observed, evolved, station_ids, station_gain, station_offset)
    wide = jnp.concatenate(
        [features, jnp.broadcast_to(target[:, None], (target.shape[0], 128))], axis=1
    )
    aug = reduce_all(contract_rows(features, wide, HIGH), groups, rows)
    posterior = solve(aug)[:, 0]
    resid = jnp.dot(features, posterior, precision=HIGH) - target
    direction = jnp.dot(w_proj.astype(jnp.float32), posterior, precision=HIGH)
    moment_term = contract_rows(hidden.astype(jnp.float32), resid[:, None], HIGH)[:, 0]
    sigmoid_pre = jax.nn.sigmoid(pre)
    slope = sigmoid_pre * (1.0 + pre * (1.0 - sigmoid_pre))
    pre_grad = (resid[:, None] * direction[None, :] * slope).astype(jnp.bfloat16)
    grad_hidden, moment = scatter_sum(normed, pre_grad, moment_term, groups, rows)
    own_moment = moment[0, : grad_hidden.shape[0]]
    grad_proj = own_moment[:, None] * posterior[None, :]
    return (grad_hidden, grad_proj)


def solution(mesh):
    return jax.shard_map(
        body,
        mesh=mesh,
        in_specs=(
            P(("grp", "row"), None),
            P(),
            P(),
            P(),
            P(("grp", "row")),
            P(("grp", "row")),
            P(("grp", "row")),
            P(),
            P(),
        ),
        out_specs=(P(("grp", "row"), None), P(("grp", "row"), None)),
        check_vma=False,
    )
```

```python
import functools

import jax
import jax.numpy as jnp
from jax import lax
from jax.experimental import pallas as pl
from jax.experimental.pallas import tpu as pltpu
from jax.sharding import PartitionSpec as P

HIGH = lax.Precision.HIGHEST
MESH = pl.DeviceIdType.MESH
VMEM = pl.BlockSpec(memory_space=pltpu.VMEM)


def forward(rows_in, norm_gain, w_hidden, w_proj):
    values = rows_in.astype(jnp.float32)
    mean_square = jnp.mean(values * values, axis=1, keepdims=True)
    normed = (values * lax.rsqrt(mean_square + 1e-06) * norm_gain).astype(jnp.bfloat16)
    pre = jnp.dot(normed, w_hidden, preferred_element_type=jnp.float32)
    hidden = (values + jax.nn.silu(pre)).astype(jnp.bfloat16)
    features = jnp.dot(hidden, w_proj, preferred_element_type=jnp.float32)
    return (normed, pre, hidden, features)


def make_target(observed, evolved, station_ids, station_gain, station_offset):
    onehot = (
        station_ids[:, None] == jnp.arange(station_gain.shape[0], dtype=jnp.int32)[None, :]
    ).astype(jnp.float32)
    gain_rows = jnp.dot(onehot, station_gain, precision=HIGH)
    offset_rows = jnp.dot(onehot, station_offset, precision=HIGH)
    return observed - gain_rows * evolved - offset_rows


def parts_of(vector):
    parts = []
    for _ in range(3):
        parts.append(lax.reduce_precision(vector, 8, 7))
        vector = vector - parts[-1]
    parts += [jnp.zeros_like(vector)] * 5
    return jnp.stack(parts).astype(jnp.bfloat16)


def contract_rows(left, right, precision=None):
    return lax.dot_general(
        left,
        right,
        (((0,), (0,)), ((), ())),
        precision=precision,
        preferred_element_type=jnp.float32,
    )


def reduce_kernel(groups, rows, part, out, half, landed, pair_sem, sems):
    chips = groups // 2 * rows
    grp, row = lax.axis_index("grp"), lax.axis_index("row")
    core = lax.rem(grp, 2)
    chip = grp // 2 * rows + row
    sibling = (grp + 1 - 2 * core, row)

    def peer(step):
        where = lax.rem(chip + step, chips)
        return where, (where // rows * 2 + core, lax.rem(where, rows))

    barrier = pltpu.get_barrier_semaphore()
    pl.semaphore_signal(barrier, inc=1, device_id=sibling, device_id_type=MESH)

    @pl.loop(1, chips)
    def _(step):
        pl.semaphore_signal(barrier, inc=1, device_id=peer(step)[1], device_id_type=MESH)

    pl.semaphore_wait(barrier, chips)

    def copy(src, dst, send_sem, recv_sem, device):
        return pltpu.make_async_remote_copy(
            src_ref=src,
            dst_ref=dst,
            send_sem=send_sem,
            recv_sem=recv_sem,
            device_id=device,
            device_id_type=MESH,
        )

    def scatter(step):
        where, device = peer(step)
        return copy(half.at[where], landed.at[step], sems.at[0, step], sems.at[1, step], device)

    def gather(step):
        own = out.at[core, chip]
        return copy(own, own, sems.at[2, step], sems.at[3, step], peer(step)[1])

    first = copy(part.at[1 - core], half, pair_sem.at[0], pair_sem.at[1], sibling)
    first.start()
    first.wait_recv()
    half[...] = half[...] + part[core]

    @pl.loop(1, chips)
    def _(step):
        scatter(step).start()

    def add(step, total):
        scatter(step).wait_recv()
        return total + landed[step]

    out[core, chip] = lax.fori_loop(1, chips, add, half[chip])

    @pl.loop(1, chips)
    def _(step):
        gather(step).start()

    @pl.loop(1, chips)
    def _(step):
        gather(step).wait_recv()

    last = copy(out.at[core], out.at[core], pair_sem.at[2], pair_sem.at[3], sibling)
    last.start()

    @pl.loop(1, chips)
    def _(step):
        scatter(step).wait_send()
        gather(step).wait_send()

    first.wait_send()
    last.wait()


def reduce_all(part, groups, rows):
    chips = groups // 2 * rows
    high, wide = part.shape
    blocks = part.reshape(2, chips, high // (2 * chips), wide)
    out = pl.pallas_call(
        functools.partial(reduce_kernel, groups, rows),
        out_shape=jax.ShapeDtypeStruct(blocks.shape, jnp.float32),
        in_specs=[VMEM],
        out_specs=VMEM,
        scratch_shapes=[pltpu.VMEM(blocks.shape[1:], jnp.float32)] * 2
        + [pltpu.SemaphoreType.DMA((4,)), pltpu.SemaphoreType.DMA((4, chips))],
        compiler_params=pltpu.CompilerParams(
            collective_id=0, has_side_effects=True, vmem_limit_bytes=16 * 2**20
        ),
    )(blocks)
    return out.reshape(high, wide)


def solve_kernel(aug, out, work):
    feat, wide = aug.shape
    rows = lax.broadcasted_iota(jnp.int32, (feat, wide), 0)
    columns = lax.broadcasted_iota(jnp.int32, (feat, wide), 1)
    work[...] = aug[...] + jnp.where(rows == columns, 1.0, 0.0)
    tall = 8
    sub = lax.broadcasted_iota(jnp.int32, (tall, 1), 0)
    for k in range(feat // tall):
        low = k * tall
        base = low // 128 * 128
        pivot = work[low : low + tall, base:]
        for i in range(tall):
            lane = low + i - base
            column = pivot[:, lane : lane + 1]
            line = pivot[i : i + 1, :] * (1.0 / column[i : i + 1, :])
            pivot = jnp.where(sub == i, line, pivot - column * line)
        for t in list(range(k + 1, feat // tall)) + list(range(k)):
            here = slice(t * tall, (t + 1) * tall)
            left = work[here, low : low + tall]
            total = work[here, base:]
            for i in range(tall):
                total = total - left[:, i : i + 1] * pivot[i : i + 1, :]
            work[here, base:] = total
        work[low : low + tall, base:] = pivot
    out[...] = work[:, feat:]


def solve(aug):
    feat, wide = aug.shape
    return pl.pallas_call(
        solve_kernel,
        out_shape=jax.ShapeDtypeStruct((feat, wide - feat), jnp.float32),
        in_specs=[VMEM],
        out_specs=VMEM,
        scratch_shapes=[pltpu.VMEM((feat, wide), jnp.float32)],
        compiler_params=pltpu.CompilerParams(vmem_limit_bytes=40 * 2**20),
    )(aug)


def scatter_kernel(
    side, depth, pieces, left, pre, resid, direction, extra, out, extra_out, right, *scratch
):
    main, small, (send_sem, recv_sem) = scratch[:6], scratch[6:12], scratch[12:]
    grp, row = lax.axis_index("grp"), lax.axis_index("row")
    core, x = lax.rem(grp, 2), grp // 2
    z, y = row // side, lax.rem(row, side)
    p = x + core * (y - x)
    q = y + core * (x - y)
    size = out.shape[1] // pieces

    def device(new_p, new_q, new_z, new_core):
        new_x = new_p + core * (new_q - new_p)
        new_y = new_q + core * (new_p - new_q)
        return (new_x * 2 + new_core, new_z * side + new_y)

    hops = [[(0, None, device(p, q, z, 1 - core))], [], [], []]
    for step in range(1, side):
        there = lax.rem(p + step, side)
        hops[1].append((step - 1, there, device(there, q, z, core)))
    for step in range(1, side):
        there = lax.rem(q + step, side)
        hops[2].append((step - 1, there, device(p, there, z, core)))
    for step in range(1, depth):
        there = lax.rem(z + step, depth)
        hops[3].append((step - 1, there, device(p, q, there, core)))

    barrier = pltpu.get_barrier_semaphore()
    for hop in sum(hops, []):
        pl.semaphore_signal(barrier, inc=1, device_id=hop[2], device_id_type=MESH)
    pl.semaphore_wait(barrier, sum(len(stage) for stage in hops))

    def copies(group, piece, stage):
        give, mine, land = group[0], group[1], group[2:]
        sem = pieces if group is small else piece
        number = sum(len(before) for before in hops[:stage])
        result = []
        for slot, there, target in hops[stage]:
            if stage == 0:
                src, dst = give.at[piece], land[0].at[piece]
            elif stage == 1:
                src, dst = mine.at[piece, there], land[1].at[piece, slot]
            elif stage == 2:
                src, dst = mine.at[piece, p, there], land[2].at[piece, slot]
            else:
                src, dst = mine.at[piece, p, q, there], land[3].at[piece, slot]
            result.append(
                pltpu.make_async_remote_copy(
                    src_ref=src,
                    dst_ref=dst,
                    send_sem=send_sem.at[sem, number + slot],
                    recv_sem=recv_sem.at[sem, number + slot],
                    device_id=target,
                    device_id_type=MESH,
                )
            )
        return result

    def begin(group, piece, stage):
        for copy in copies(group, piece, stage):
            copy.start()

    def finish(group, piece, stage):
        mine, land = group[1], group[2:]
        for copy in copies(group, piece, stage):
            copy.wait_recv()
        if stage == 0:
            mine[piece] = mine[piece] + land[0][piece]
        elif stage == 1:
            for slot in range(side - 1):
                mine[piece, p] = mine[piece, p] + land[1][piece, slot]
        elif stage == 2:
            for slot in range(side - 1):
                mine[piece, p, q] = mine[piece, p, q] + land[2][piece, slot]
        else:
            total = mine[piece, p, q, z]
            for slot in range(depth - 1):
                total = total + land[3][piece, slot]
            if group is small:
                extra_out[...] = total
            else:
                out[:, pl.ds(pl.multiple_of(piece * size, size), size)] = total
        if stage < 3:
            begin(group, piece, stage + 1)

    def product(half, piece, into):
        into[piece] = jnp.dot(
            left[half], right[...], preferred_element_type=jnp.float32
        ).reshape(into.shape[1:])

    small[0][0] = extra[1 - core]
    small[1][0] = extra[core]
    begin(small, 0, 0)

    @pl.loop(0, pieces)
    def _(piece):
        columns = pl.ds(pl.multiple_of(piece * size, size), size)
        value = pre[:, columns]
        sigmoid = 1.0 / (1.0 + jnp.exp(-value))
        slope = sigmoid * (1.0 + value * (1.0 - sigmoid))
        right[...] = (resid[...] * direction[:, columns] * slope).astype(jnp.bfloat16)
        product(1 - core, piece, main[0])
        begin(main, piece, 0)
        product(core, piece, main[1])

        @pl.when(piece > 0)
        def _():
            finish(main, piece - 1, 0)

    finish(main, pieces - 1, 0)
    finish(small, 0, 0)
    finish(small, 0, 1)

    @pl.loop(0, pieces)
    def _(piece):
        finish(main, piece, 1)

        @pl.when(piece > 0)
        def _():
            finish(main, piece - 1, 2)

    finish(main, pieces - 1, 2)
    finish(small, 0, 2)
    finish(small, 0, 3)

    @pl.loop(0, pieces)
    def _(piece):
        finish(main, piece, 3)

    for stage in range(4):
        for copy in copies(small, 0, stage):
            copy.wait_send()

    @pl.loop(0, pieces)
    def _(piece):
        for stage in range(4):
            for copy in copies(main, piece, stage):
                copy.wait_send()


def order_rows(array, side, depth):
    tail = array.shape[1:]
    split = array.reshape((side, 2, depth, side, -1) + tail)
    rest = tuple(range(3, split.ndim - 1))
    first = jnp.transpose(split[:, 0], (0, 2, 1) + rest)
    second = jnp.transpose(split[:, 1], (2, 0, 1) + rest)
    return jnp.stack([first, second])


def scatter_sum(normed, pre, resid, direction, moment_term, groups, rows):
    side = groups // 2
    depth = rows // side
    own = normed.shape[1] // (groups * rows)
    width = pre.shape[1]
    pieces = width // 128
    left = order_rows(normed.T, side, depth).reshape(2, -1, normed.shape[0])
    extra = order_rows(moment_term, side, depth)[..., None, :]
    extra = jnp.pad(extra, [(0, 0)] * 4 + [(0, 7), (0, 128 - own)])

    def stage_buffers(count, high, wide):
        full = (count, side, side, depth, high, wide)
        shapes = [full] * 3 + [
            (count, side - 1, side, depth, high, wide),
            (count, side - 1, depth, high, wide),
            (count, depth - 1, high, wide),
        ]
        return [pltpu.VMEM(shape, jnp.float32) for shape in shapes]

    number = 1 + 2 * (side - 1) + depth - 1
    return pl.pallas_call(
        functools.partial(scatter_kernel, side, depth, pieces),
        out_shape=(
            jax.ShapeDtypeStruct((own, width), jnp.float32),
            jax.ShapeDtypeStruct((8, 128), jnp.float32),
        ),
        in_specs=[VMEM] * 5,
        out_specs=(VMEM, VMEM),
        scratch_shapes=[pltpu.VMEM((pre.shape[0], width // pieces), jnp.bfloat16)]
        + stage_buffers(pieces, own, width // pieces)
        + stage_buffers(1, 8, 128)
        + [pltpu.SemaphoreType.DMA((pieces + 1, number))] * 2,
        compiler_params=pltpu.CompilerParams(
            collective_id=1, has_side_effects=True, vmem_limit_bytes=56 * 2**20
        ),
    )(left, pre, resid[:, None], direction[None, :], extra)


def body(
    inputs,
    norm_gain,
    w_hidden,
    w_proj,
    observed,
    evolved,
    station_ids,
    station_gain,
    station_offset,
):
    groups, rows = lax.axis_size("grp"), lax.axis_size("row")
    feat_width = w_proj.shape[1]
    normed, pre, hidden, features = forward(inputs, norm_gain, w_hidden, w_proj)
    target = make_target(observed, evolved, station_ids, station_gain, station_offset)
    wide = jnp.concatenate(
        [features, jnp.broadcast_to(target[:, None], (target.shape[0], 128))], axis=1
    )
    aug = reduce_all(contract_rows(features, wide, HIGH), groups, rows)
    posterior = solve(aug)[:, 0]
    resid = jnp.dot(features, posterior, precision=HIGH) - target
    direction = jnp.sum(
        lax.dot_general(
            parts_of(posterior), w_proj, (((1,), (1,)), ((), ())), preferred_element_type=jnp.float32
        ),
        axis=0,
    )
    moment_term = jnp.sum(
        jnp.dot(parts_of(resid), hidden, preferred_element_type=jnp.float32), axis=0
    )
    grad_hidden, moment = scatter_sum(
        normed, pre, resid, direction, moment_term, groups, rows
    )
    own_moment = moment[0, : grad_hidden.shape[0]]
    grad_proj = own_moment[:, None] * posterior[None, :]
    return (grad_hidden, grad_proj)


def solution(mesh):
    return jax.shard_map(
        body,
        mesh=mesh,
        in_specs=(
            P(("grp", "row"), None),
            P(),
            P(),
            P(),
            P(("grp", "row")),
            P(("grp", "row")),
            P(("grp", "row")),
            P(),
            P(),
        ),
        out_specs=(P(("grp", "row"), None), P(("grp", "row"), None)),
        check_vma=False,
    )
```
